32 devices in a mesh: seq: 8 (over z, x), mp: 4 (over y, core).
Axes of the slice: x: 2, y: 2, z: 4, core: 2. Of those that a mesh axis runs over, the one named last changes fastest.
Arguments:
- hidden: bfloat16 [4096, 4096], P('seq', 'mp'), may hold values from -6 to 6
- w_zx: bfloat16 [4096, 2, 4096], P(None, None, 'mp'), may hold values from -0.09375 to 0.09375
- w_bc: bfloat16 [4096, 2, 512], P(None, None, 'mp'), may hold values from -0.09375 to 0.09375
- w_dt: bfloat16 [4096, 64], P(None, 'mp'), may hold values from -0.09375 to 0.09375
- conv_x: float32 [4, 4096], P(None, 'mp'), may hold values from -3 to 3
- conv_x_bias: float32 [4096], P('mp'), may hold values from -3 to 3
- conv_bc: float32 [4, 2, 512], P(None, None, 'mp'), may hold values from -3 to 3
- conv_bc_bias: float32 [2, 512], P(None, 'mp'), may hold values from -3 to 3
- a_log: float32 [64], P('mp'), may hold values from -9.5 to -0.5
- dt_bias: float32 [64], P('mp'), may hold values from -4 to -1
- d_skip: float32 [64], P('mp'), may hold values from 0.5 to 4
- norm_gain: float32 [4096], P('mp'), may hold values from 0.4 to 1.6
- state_bank: float32 [2, 64, 64, 128], P(None, 'mp'), may hold values from -2 to 2
- conv_bank_x: bfloat16 [2, 3, 4096], P(None, None, 'mp'), may hold values from -5 to 5
- conv_bank_bc: bfloat16 [2, 3, 2, 512], P(None, None, None, 'mp'), may hold values from -5 to 5
- prompt_blocks: int32 [3], replicated, may hold values from 1 to 12, 16 in all
- prompt_order: int32 [3], replicated, may hold values from 0 to 2, each once
- resume_slot: int32 [3], replicated, may hold values from 0 to 2
Outputs:
- mixed: bfloat16 [4096, 4096], P('seq', 'mp')
The draws below stay inside these ranges and needn't reach their ends.
Inputs may be any that keep to these rules, and one draw needn't show every extreme that they name: `prompt_blocks`: blocks of each prompt; they sum to 16 and the longest is exactly 12. `prompt_order`: A permutation of the prompts. `resume_slot`: 2 means a fresh start from zero state and zero convolution rows.
All inputs are finite; a program needn't handle non-finite values.
Results may differ from the reference program's by a relative error of at most 0.0068.
Values may be sent and summed in bfloat16 or wider, within the bound.
A program may use at most 192 MiB of HBM per device.

```python
import math
import jax
import jax.numpy as jnp
import numpy as np
from jax import lax

WIDTH = 4096
HEADS = 64
HEAD_DIM = 64
GROUPS = 4
STATE = 128
BLOCK = 256
KERNEL = 4
BLOCKS_DEV = 2
BANK = 2
INNER = 4096
GROUP_STATE = 512
NBLOCKS = 16
TOKENS = 4096
PROMPTS = 3
LONGEST = 12
N_SEQ = 8


def draw_a_log(key, part):
    key_slow = jax.random.fold_in(key, 11)
    key_fast = jax.random.fold_in(key, 12)
    key_pick = jax.random.fold_in(key, 13)
    slow = jax.random.uniform(key_slow, (HEADS,), jnp.float32, -9.5, -3.5)
    fast = jax.random.uniform(key_fast, (HEADS,), jnp.float32, -2.0, -0.5)
    chosen = jax.random.randint(key_pick, (HEADS // 8, 1), 0, 8)
    marked = (jnp.arange(8, dtype=jnp.int32)[None, :] == chosen).reshape(HEADS)
    return jnp.where(marked, fast, slow)


def steps_of(rng, dims, shards, least, largest):
    factor_of, own = 1.0, jax.random.fold_in(rng, 6)
    for position, blocks in shards:
        draws = jnp.exp(jax.random.uniform(jax.random.fold_in(own, position), (blocks,), jnp.float32, least / len(shards), largest / len(shards)))
        factor_of = factor_of * jnp.repeat(draws, dims[position] // blocks).reshape([-1 if axis == position else 1 for axis in range(len(dims))])
    return factor_of


def profile(amount, total, bound, skew):
    portions = [(1 << 20) // math.isqrt(grade ** skew) + 1 for grade in range(2, amount + 1)]
    spare, counts = total - bound - (amount - 1), [1] * (amount - 1)
    while spare > 0:
        movable = [i for i in range(amount - 1) if counts[i] < bound]
        whole, left = sum([portions[i] for i in movable]), spare
        for i in movable:
            addition = min(bound - counts[i], max(1, left * portions[i] // whole), spare)
            counts[i] = counts[i] + addition
            spare = spare - addition
    return np.array([bound] + counts)


def ragged(stream_key, amount, total, reach, skew):
    if amount == 2:
        one = jax.random.randint(stream_key, (), max(1, total - reach), min(reach, total - 1) + 1)
        return jnp.stack([one, total - one])
    sizes = jnp.asarray(profile(amount, total, reach, skew), jnp.int32)
    pairs = (amount - 1) // 2
    source_of, receiver = sizes[1:1 + 2 * pairs:2], sizes[2:2 + 2 * pairs:2]
    slack = jnp.minimum(source_of - 1, reach - receiver)
    passed = jax.random.randint(jax.random.fold_in(stream_key, 1), (pairs,), 0, 1 << 20) % (slack + 1)
    sizes = sizes.at[1:1 + 2 * pairs:2].set(source_of - passed).at[2:2 + 2 * pairs:2].set(receiver + passed)
    return sizes[jax.random.permutation(jax.random.fold_in(stream_key, 2), amount)]


def gaussian(rng, shape, width, most, shards=(), kind=jnp.bfloat16):
    array = jax.random.normal(rng, shape, jnp.float32) * width
    if len(shards) > 0:
        array = steps_of(rng, shape, shards, -0.22, 0.18) * array
    return jnp.clip(array, min=-most, max=most).astype(kind)


def setup_inputs(seed: int = 0) -> dict:
    keys = jax.random.split(jax.random.key(seed), 19)
    hidden = gaussian(keys[0], (TOKENS, WIDTH), 1.0, 6.0, ((0, 8), (1, 4)))
    w_zx = gaussian(keys[1], (WIDTH, 2, INNER), WIDTH ** -0.5, 0.09375, ((2, 4),))
    w_bc = gaussian(keys[2], (WIDTH, 2, GROUP_STATE), WIDTH ** -0.5, 0.09375, ((2, 4),))
    w_dt = gaussian(keys[3], (WIDTH, HEADS), WIDTH ** -0.5, 0.09375, ((1, 4),))
    conv_x = gaussian(keys[4], (KERNEL, INNER), KERNEL ** -0.5, 3.0, ((1, 4),), jnp.float32)
    conv_x_bias = gaussian(keys[5], (INNER,), 0.5, 3.0, ((0, 4),), jnp.float32)
    conv_bc = gaussian(keys[6], (KERNEL, 2, GROUP_STATE), KERNEL ** -0.5, 3.0, ((2, 4),), jnp.float32)
    conv_bc_bias = gaussian(keys[7], (2, GROUP_STATE), 0.5, 3.0, ((1, 4),), jnp.float32)
    a_log = draw_a_log(jax.random.fold_in(keys[18], 71), 0)
    dt_bias = jnp.clip(-4.0 + 3.0 * jax.random.uniform(keys[9], (HEADS,), jnp.float32) ** steps_of(keys[9], (HEADS,), ((0, 4),), -0.2, 0.2), -4.0, -1.0)
    d_skip = jnp.clip(0.5 + 3.5 * jax.random.uniform(keys[10], (HEADS,), jnp.float32) ** steps_of(keys[10], (HEADS,), ((0, 4),), -0.2, 0.2), 0.5, 4.0)
    norm_gain = jnp.clip(1.0 + 0.12 * jax.random.normal(keys[11], (INNER,), jnp.float32), 0.4, 1.6)
    state_bank = gaussian(keys[12], (BANK, HEADS, HEAD_DIM, STATE), 0.3, 2.0, ((1, 4),), jnp.float32)
    conv_bank_x = gaussian(keys[13], (BANK, KERNEL - 1, INNER), 1.0, 5.0, ((2, 4),))
    conv_bank_bc = gaussian(keys[14], (BANK, KERNEL - 1, 2, GROUP_STATE), 1.0, 5.0, ((3, 4),))
    prompt_blocks = ragged(keys[15], PROMPTS, NBLOCKS, LONGEST, 2).astype(jnp.int32)
    prompt_order = jax.random.permutation(keys[16], PROMPTS).astype(jnp.int32)
    resume_slot = jax.random.randint(keys[17], (PROMPTS,), 0, BANK + 1).astype(jnp.int32)
    return dict(hidden=hidden, w_zx=w_zx, w_bc=w_bc, w_dt=w_dt, conv_x=conv_x, conv_x_bias=conv_x_bias, conv_bc=conv_bc, conv_bc_bias=conv_bc_bias, a_log=a_log, dt_bias=dt_bias, d_skip=d_skip, norm_gain=norm_gain, state_bank=state_bank, conv_bank_x=conv_bank_x, conv_bank_bc=conv_bank_bc, prompt_blocks=prompt_blocks, prompt_order=prompt_order, resume_slot=resume_slot)


def reference(hidden, w_zx, w_bc, w_dt, conv_x, conv_x_bias, conv_bc, conv_bc_bias, a_log, dt_bias, d_skip, norm_gain, state_bank, conv_bank_x, conv_bank_bc, prompt_blocks, prompt_order, resume_slot):
    per_group = HEADS // GROUPS
    stream = hidden.reshape(N_SEQ, BLOCKS_DEV, BLOCK, WIDTH).transpose(1, 0, 2, 3).reshape(NBLOCKS, BLOCK, WIDTH)
    lengths = prompt_blocks[prompt_order].astype(jnp.int32)
    ends = jnp.cumsum(lengths).astype(jnp.int32)
    starts = (ends - lengths).astype(jnp.int32)
    slots = resume_slot[prompt_order].astype(jnp.int32)
    block_ids = jnp.arange(NBLOCKS, dtype=jnp.int32)
    owner = lax.optimization_barrier(jnp.sum((block_ids[:, None] >= ends[None, :]).astype(jnp.int32), axis=1)).astype(jnp.int32)
    first = jnp.any(block_ids[:, None] == starts[None, :], axis=1)
    block_slot = slots[owner]
    flat_zx = w_zx.reshape(WIDTH, 2 * INNER)
    flat_bc = w_bc.reshape(WIDTH, 2 * GROUP_STATE)
    kernel = jnp.concatenate([conv_x, conv_bc.reshape(KERNEL, 2 * GROUP_STATE)], axis=1).astype(jnp.float32)
    bias = jnp.concatenate([conv_x_bias, conv_bc_bias.reshape(2 * GROUP_STATE)], axis=0).astype(jnp.float32)
    bank_tails = jnp.concatenate([conv_bank_x, conv_bank_bc.reshape(BANK, KERNEL - 1, 2 * GROUP_STATE)], axis=2)
    rates = -jnp.exp(a_log)
    lower = jnp.arange(BLOCK)[:, None] >= jnp.arange(BLOCK)[None, :]
    head_group = jnp.arange(HEADS) // per_group

    def one_block(carry, inputs):
        state_prev, tail_prev = carry
        rows, is_first, slot = inputs
        zx = jnp.dot(rows, flat_zx, preferred_element_type=jnp.float32).astype(jnp.bfloat16)
        bc = jnp.dot(rows, flat_bc, preferred_element_type=jnp.float32).astype(jnp.bfloat16)
        dt_raw = jnp.dot(rows, w_dt, preferred_element_type=jnp.float32)
        gate = zx[:, :INNER]
        mixin = jnp.concatenate([zx[:, INNER:], bc], axis=1)
        pick = (slot == jnp.arange(BANK, dtype=jnp.int32)).astype(jnp.float32)
        bank_tail = jnp.einsum('r,rkz->kz', pick, bank_tails.astype(jnp.float32)).astype(jnp.bfloat16)
        init = jnp.einsum('r,rhpn->hpn', pick, state_bank, precision=lax.Precision.HIGHEST)
        tail = jnp.where(is_first, bank_tail, tail_prev)
        state_in = jnp.where(is_first, init, state_prev)
        padded = jnp.concatenate([tail, mixin], axis=0).astype(jnp.float32)
        acc = bias[None, :] + padded[0:BLOCK] * kernel[0]
        for k in range(1, KERNEL):
            acc = acc + padded[k:k + BLOCK] * kernel[k]
        conv = jax.nn.silu(acc).astype(jnp.bfloat16)
        xs = conv[:, :INNER].reshape(BLOCK, HEADS, HEAD_DIM)
        bs = conv[:, INNER:INNER + GROUP_STATE].reshape(BLOCK, GROUPS, STATE)
        cq = conv[:, INNER + GROUP_STATE:].reshape(BLOCK, GROUPS, STATE)
        dt = jax.nn.softplus(dt_raw + dt_bias[None, :])
        cum = jnp.cumsum(dt * rates[None, :], axis=0)
        scores = jnp.einsum('qgn,kgn->gqk', cq.astype(jnp.float32), bs.astype(jnp.float32))
        cum_h = cum.T
        diff = cum_h[:, :, None] - cum_h[:, None, :]
        damp = jnp.exp(jnp.where(lower[None], diff, -jnp.inf))
        mix = (scores[head_group] * damp * dt.T[:, None, :]).astype(jnp.bfloat16)
        y_intra = jnp.einsum('hqk,khp->qhp', mix.astype(jnp.float32), xs.astype(jnp.float32))
        last = cum[-1]
        read = jnp.einsum('qgn,gjpn->qgjp', cq.astype(jnp.float32), state_in.reshape(GROUPS, per_group, HEAD_DIM, STATE), precision=lax.Precision.HIGHEST).reshape(BLOCK, HEADS, HEAD_DIM)
        y = y_intra + jnp.exp(cum)[:, :, None] * read + d_skip[None, :, None] * xs.astype(jnp.float32)
        weighted = (xs.astype(jnp.float32) * (dt * jnp.exp(last[None, :] - cum))[:, :, None]).astype(jnp.bfloat16)
        local_state = jnp.einsum('qgjp,qgn->gjpn', weighted.reshape(BLOCK, GROUPS, per_group, HEAD_DIM).astype(jnp.float32), bs.astype(jnp.float32)).reshape(HEADS, HEAD_DIM, STATE)
        state_end = jnp.exp(last)[:, None, None] * state_in + local_state
        gated = y.reshape(BLOCK, INNER) * jax.nn.silu(gate.astype(jnp.float32))
        grouped = gated.reshape(BLOCK, GROUPS, INNER // GROUPS)
        scale = lax.rsqrt(lax.optimization_barrier(jnp.mean(grouped * grouped, axis=2, keepdims=True)) + 1e-05)
        out = (grouped * scale).reshape(BLOCK, INNER) * norm_gain[None, :]
        return ((state_end, mixin[BLOCK - (KERNEL - 1):]), out.astype(jnp.bfloat16))
    start = (jnp.zeros((HEADS, HEAD_DIM, STATE), jnp.float32), jnp.zeros((KERNEL - 1, INNER + 2 * GROUP_STATE), jnp.bfloat16))
    _, outs = lax.scan(one_block, start, (stream, first, block_slot))
    return outs.reshape(BLOCKS_DEV, N_SEQ, BLOCK, INNER).transpose(1, 0, 2, 3).reshape(TOKENS, INNER)
```

```python
import functools

import jax
import jax.numpy as jnp
from jax import lax
from jax.experimental import pallas as pl
from jax.experimental.pallas import tpu as pltpu
from jax.sharding import PartitionSpec as P

WIDTH = 4096
HEAD_DIM = 64
STATE = 128
BLOCK = 256
KERNEL = 4
BANK = 2


def from_behind(value, axis, steps):
    count = lax.axis_size(axis)
    pairs = [(source, (source + steps) % count) for source in range(count)]
    return lax.ppermute(value, axis, pairs)


def exchange_kernel(
    count, blocks, local_ref, grow_ref, pick_ref, bank_ref, out_ref,
    got, back, grown, send_a, recv_a, send_g, recv_g, send_b, recv_b,
):
    me = lax.axis_index("seq")
    barrier = pltpu.get_barrier_semaphore()
    for k in range(1, count):
        pl.semaphore_signal(
            barrier,
            inc=1,
            device_id={"seq": lax.rem(me + k, count)},
            device_id_type=pl.DeviceIdType.MESH,
        )
    pl.semaphore_wait(barrier, count - 1)
    outward = []
    for k in range(1, count):
        peer = lax.rem(me + k, count)
        for src, dst, send, recv in (
            (grow_ref, grown, send_g, recv_g),
            (local_ref, got, send_a, recv_a),
        ):
            copy = pltpu.make_async_remote_copy(
                src_ref=src.at[peer],
                dst_ref=dst.at[me],
                send_sem=send.at[k - 1],
                recv_sem=recv.at[k - 1],
                device_id={"seq": peer},
                device_id_type=pl.DeviceIdType.MESH,
            )
            copy.start()
            outward.append(copy)
    got[me] = local_ref[me]
    grown[me] = grow_ref[me]
    for copy in outward:
        copy.wait()
    rows = local_ref.shape[2]
    parts = max(rows // HEAD_DIM, 1)
    span = rows // parts
    for part in range(parts):
        here = slice(part * span, (part + 1) * span)
        state = jnp.zeros((span, STATE), jnp.float32)
        for c in range(count * blocks):
            device, row = c % count, c // count
            state = pick_ref[c, 0:1, :] * state
            for r in range(BANK):
                state = state + pick_ref[c, 1 + r : 2 + r, :] * bank_ref[r, here, :]
            back[device, row, here, :] = state.astype(jnp.bfloat16)
            at = row * parts + part
            state = grown[device, at : at + 1, :] * state + got[device, row, here, :].astype(
                jnp.float32
            )
    homeward = []
    for k in range(1, count):
        peer = lax.rem(me + k, count)
        copy = pltpu.make_async_remote_copy(
            src_ref=back.at[peer],
            dst_ref=out_ref.at[me],
            send_sem=send_b.at[k - 1],
            recv_sem=recv_b.at[k - 1],
            device_id={"seq": peer},
            device_id_type=pl.DeviceIdType.MESH,
        )
        copy.start()
        homeward.append(copy)
    out_ref[me] = back[me]
    for copy in homeward:
        copy.wait()


def entering_states(local_state, grow, pick, first, bank, place, count):
    blocks, rows_all, _ = local_state.shape
    heads = grow.shape[1]
    rows = rows_all // count
    local = local_state.astype(jnp.bfloat16).reshape(blocks, count, rows, STATE)
    local = local.transpose(1, 0, 2, 3)
    if heads < count:
        grow = jnp.repeat(grow, count // heads, axis=1)
    grow = grow.reshape(blocks, count, -1).transpose(1, 0, 2).reshape(count, -1)
    padded = -(-grow.shape[1] // 8) * 8
    grow = jnp.pad(grow, ((0, 0), (0, padded - grow.shape[1])))
    grow = jnp.broadcast_to(grow[:, :, None], (count, padded, STATE))
    picks = jnp.concatenate([1.0 - first[:, None], first[:, None] * pick], axis=1)
    picks = jnp.pad(picks, ((0, 0), (0, 8 - picks.shape[1])))
    picks = jnp.broadcast_to(picks[:, :, None], (count * blocks, 8, STATE))
    mine = lax.dynamic_slice_in_dim(bank, place * rows, rows, axis=1)
    dma = pltpu.SemaphoreType.DMA((count - 1,))
    out = pl.pallas_call(
        functools.partial(exchange_kernel, count, blocks),
        out_shape=jax.ShapeDtypeStruct((count, blocks, rows, STATE), jnp.bfloat16),
        in_specs=[pl.BlockSpec(memory_space=pltpu.VMEM)] * 4,
        out_specs=pl.BlockSpec(memory_space=pltpu.VMEM),
        scratch_shapes=[
            pltpu.VMEM((count, blocks, rows, STATE), jnp.bfloat16),
            pltpu.VMEM((count, blocks, rows, STATE), jnp.bfloat16),
            pltpu.VMEM((count, padded, STATE), jnp.float32),
            dma, dma, dma, dma, dma, dma,
        ],
        compiler_params=pltpu.CompilerParams(collective_id=0, has_side_effects=True),
        name="exchange",
    )(local, grow, picks, mine)
    return out.transpose(1, 0, 2, 3).reshape(blocks, rows_all, STATE)


def swap(value, axis, bit):
    count = lax.axis_size(axis)
    return lax.ppermute(value, axis, [(source, source ^ bit) for source in range(count)])


def gather_columns(rows, axis):
    mine, width = lax.axis_index(axis), rows.shape[1]
    far = swap(rows, axis, 2)
    near = swap(rows, axis, 1)
    both = swap(far, axis, 1)
    whole = jnp.zeros((rows.shape[0], width * 4), rows.dtype)
    for bits, part in ((0, rows), (1, near), (2, far), (3, both)):
        whole = lax.dynamic_update_slice_in_dim(whole, part, (mine ^ bits) * width, axis=1)
    return whole


def per_device(
    hidden,
    w_zx,
    w_bc,
    w_dt,
    conv_x,
    conv_x_bias,
    conv_bc,
    conv_bc_bias,
    a_log,
    dt_bias,
    d_skip,
    norm_gain,
    state_bank,
    conv_bank_x,
    conv_bank_bc,
    prompt_blocks,
    prompt_order,
    resume_slot,
):
    devices = lax.axis_size("seq")
    place = lax.axis_index("seq")
    rows_dev = hidden.shape[0]
    blocks = rows_dev // BLOCK
    inner_dev = w_zx.shape[2]
    gstate_dev = w_bc.shape[2]
    heads_dev = w_dt.shape[1]
    groups_dev = gstate_dev // STATE
    per_group = heads_dev // groups_dev
    channels = inner_dev + 2 * gstate_dev
    prompts = prompt_blocks.shape[0]
    flat_zx = w_zx.reshape(WIDTH, 2 * inner_dev)
    flat_bc = w_bc.reshape(WIDTH, 2 * gstate_dev)
    pieces = []
    for row in range(blocks):
        pieces.append(gather_columns(hidden[row * BLOCK : (row + 1) * BLOCK], "mp"))
    zx, bc, dt_raw = [], [], []
    for piece in pieces:
        zx.append(jnp.dot(piece, flat_zx, preferred_element_type=jnp.float32).astype(jnp.bfloat16))
        bc.append(jnp.dot(piece, flat_bc, preferred_element_type=jnp.float32).astype(jnp.bfloat16))
        dt_raw.append(jnp.dot(piece, w_dt, preferred_element_type=jnp.float32))
    zx, bc, dt_raw = (jnp.concatenate(parts, axis=0) for parts in (zx, bc, dt_raw))
    gate = zx[:, :inner_dev]
    mixin = jnp.concatenate([zx[:, inner_dev:], bc], axis=1).reshape(blocks, BLOCK, channels)
    own_tails = mixin[:, BLOCK - (KERNEL - 1) :, :]
    arrived = from_behind(own_tails, "seq", 1)
    wrapped = jnp.concatenate([jnp.zeros_like(arrived[:1]), arrived[:-1]], axis=0)
    before = jnp.where(place > 0, arrived, wrapped)
    prompt_ids = jnp.arange(prompts, dtype=jnp.int32)
    order_hot = (prompt_order[:, None] == prompt_ids[None, :]).astype(jnp.int32)
    lengths = jnp.sum(order_hot * prompt_blocks[None, :], axis=1)
    slots = jnp.sum(order_hot * resume_slot[None, :], axis=1)
    ends = jnp.cumsum(lengths)
    starts = ends - lengths
    every_id = jnp.arange(blocks * devices, dtype=jnp.int32)
    inside = (
        (every_id[:, None] >= starts[None, :]) & (every_id[:, None] < ends[None, :])
    ).astype(jnp.int32)
    every_slot = jnp.sum(inside * slots[None, :], axis=1)
    every_first = jnp.any(every_id[:, None] == starts[None, :], axis=1).astype(jnp.float32)
    every_pick = (
        every_slot[:, None] == jnp.arange(BANK, dtype=jnp.int32)[None, :]
    ).astype(jnp.float32)
    stream_ids = jnp.arange(blocks, dtype=jnp.int32) * devices + place
    first = jnp.any(stream_ids[:, None] == starts[None, :], axis=1)
    block_slot = jnp.sum(
        jnp.where(stream_ids[:, None] == every_id[None, :], every_slot[None, :], 0), axis=1
    )
    pick = (block_slot[:, None] == jnp.arange(BANK, dtype=jnp.int32)[None, :]).astype(jnp.float32)
    bank_rows = jnp.concatenate(
        [conv_bank_x, conv_bank_bc.reshape(BANK, KERNEL - 1, 2 * gstate_dev)], axis=2
    )
    bank_tail = jnp.einsum("cr,rkz->ckz", pick, bank_rows.astype(jnp.float32)).astype(jnp.bfloat16)
    tail = jnp.where(first[:, None, None], bank_tail, before)
    kernel = jnp.concatenate([conv_x, conv_bc.reshape(KERNEL, 2 * gstate_dev)], axis=1)
    bias = jnp.concatenate([conv_x_bias, conv_bc_bias.reshape(2 * gstate_dev)], axis=0)
    padded = jnp.concatenate([tail, mixin], axis=1).astype(jnp.float32)
    acc = bias[None, None, :] + padded[:, 0:BLOCK] * kernel[0]
    for k in range(1, KERNEL):
        acc = acc + padded[:, k : k + BLOCK] * kernel[k]
    conv = jax.nn.silu(acc).astype(jnp.bfloat16)
    xs = conv[..., :inner_dev].reshape(blocks, BLOCK, groups_dev, per_group, HEAD_DIM)
    bs = conv[..., inner_dev : inner_dev + gstate_dev].reshape(blocks, BLOCK, groups_dev, STATE)
    cq = conv[..., inner_dev + gstate_dev :].reshape(blocks, BLOCK, groups_dev, STATE)
    dt = jax.nn.softplus(dt_raw.reshape(blocks, BLOCK, heads_dev) + dt_bias[None, None, :])
    cum = jnp.cumsum(dt * (-jnp.exp(a_log))[None, None, :], axis=1)
    scores = jnp.einsum("cqgn,ckgn->cgqk", cq, bs, preferred_element_type=jnp.float32)
    cum_h = cum.transpose(0, 2, 1)
    lower = jnp.arange(BLOCK)[:, None] >= jnp.arange(BLOCK)[None, :]
    damp = jnp.exp(
        jnp.where(lower[None, None], cum_h[:, :, :, None] - cum_h[:, :, None, :], -jnp.inf)
    )
    damp = damp.reshape(blocks, groups_dev, per_group, BLOCK, BLOCK)
    dt_h = dt.transpose(0, 2, 1).reshape(blocks, groups_dev, per_group, 1, BLOCK)
    mix = (scores[:, :, None] * damp * dt_h).astype(jnp.bfloat16)
    y_intra = jnp.einsum("cgjqk,ckgjp->cqgjp", mix, xs, preferred_element_type=jnp.float32)
    last = cum[:, -1, :]
    grow = jnp.exp(last)
    factor = (dt * jnp.exp(last[:, None, :] - cum)).reshape(blocks, BLOCK, groups_dev, per_group, 1)
    weighted = (xs.astype(jnp.float32) * factor).astype(jnp.bfloat16)
    local_state = jnp.einsum(
        "cqgjp,cqgn->cgjpn", weighted, bs, preferred_element_type=jnp.float32
    ).reshape(blocks, heads_dev, HEAD_DIM, STATE)
    state_in = entering_states(
        local_state.reshape(blocks, heads_dev * HEAD_DIM, STATE),
        grow,
        every_pick,
        every_first,
        state_bank.reshape(BANK, heads_dev * HEAD_DIM, STATE),
        place,
        devices,
    )
    read = jnp.einsum(
        "cqgn,cgjpn->cqgjp",
        cq,
        state_in.reshape(blocks, groups_dev, per_group, HEAD_DIM, STATE),
        preferred_element_type=jnp.float32,
    )
    growth = jnp.exp(cum).reshape(blocks, BLOCK, groups_dev, per_group, 1)
    skip = d_skip.reshape(1, 1, groups_dev, per_group, 1)
    y_total = y_intra + growth * read + skip * xs.astype(jnp.float32)
    gated = y_total.reshape(rows_dev, inner_dev) * jax.nn.silu(gate.astype(jnp.float32))
    grouped = gated.reshape(rows_dev, groups_dev, inner_dev // groups_dev)
    scale = lax.rsqrt(jnp.mean(grouped * grouped, axis=2, keepdims=True) + 1e-05)
    result = (grouped * scale).reshape(rows_dev, inner_dev) * norm_gain[None, :]
    return result.astype(jnp.bfloat16)


def solution(mesh):
    placed = (
        P("seq", "mp"),
        P(None, None, "mp"),
        P(None, None, "mp"),
        P(None, "mp"),
        P(None, "mp"),
        P("mp"),
        P(None, None, "mp"),
        P(None, "mp"),
        P("mp"),
        P("mp"),
        P("mp"),
        P("mp"),
        P(None, "mp", None, None),
        P(None, None, "mp"),
        P(None, None, None, "mp"),
        P(),
        P(),
        P(),
    )
    return jax.shard_map(
        per_device, mesh=mesh, in_specs=placed, out_specs=P("seq", "mp"), check_vma=False
    )
```

```python
import functools

import jax
import jax.numpy as jnp
from jax import lax
from jax.experimental import pallas as pl
from jax.experimental.pallas import tpu as pltpu
from jax.sharding import PartitionSpec as P

WIDTH = 4096
HEAD_DIM = 64
STATE = 128
BLOCK = 256
KERNEL = 4
BANK = 2


def from_behind(value, axis, steps):
    count = lax.axis_size(axis)
    pairs = [(source, (source + steps) % count) for source in range(count)]
    return lax.ppermute(value, axis, pairs)


def exchange_kernel(
    count, blocks, local_ref, grow_ref, pick_ref, bank_ref, out_ref,
    got, back, grown, send_a, recv_a, send_g, recv_g, send_b, recv_b,
):
    me = lax.axis_index("seq")
    barrier = pltpu.get_barrier_semaphore()
    for k in range(1, count):
        pl.semaphore_signal(
            barrier,
            inc=1,
            device_id={"seq": lax.rem(me + k, count)},
            device_id_type=pl.DeviceIdType.MESH,
        )
    pl.semaphore_wait(barrier, count - 1)
    outward = []
    for k in range(1, count):
        peer = lax.rem(me + k, count)
        for src, dst, send, recv in (
            (grow_ref, grown, send_g, recv_g),
            (local_ref, got, send_a, recv_a),
        ):
            copy = pltpu.make_async_remote_copy(
                src_ref=src.at[peer],
                dst_ref=dst.at[me],
                send_sem=send.at[k - 1],
                recv_sem=recv.at[k - 1],
                device_id={"seq": peer},
                device_id_type=pl.DeviceIdType.MESH,
            )
            copy.start()
            outward.append(copy)
    got[me] = local_ref[me]
    grown[me] = grow_ref[me]
    for copy in outward:
        copy.wait()
    rows = local_ref.shape[2]
    parts = max(rows // HEAD_DIM, 1)
    span = rows // parts
    for part in range(parts):
        here = slice(part * span, (part + 1) * span)
        state = jnp.zeros((span, STATE), jnp.float32)
        for c in range(count * blocks):
            device, row = c % count, c // count
            state = pick_ref[c, 0:1, :] * state
            for r in range(BANK):
                state = state + pick_ref[c, 1 + r : 2 + r, :] * bank_ref[r, here, :]
            back[device, row, here, :] = state.astype(jnp.bfloat16)
            at = row * parts + part
            state = grown[device, at : at + 1, :] * state + got[device, row, here, :].astype(
                jnp.float32
            )
    homeward = []
    for k in range(1, count):
        peer = lax.rem(me + k, count)
        copy = pltpu.make_async_remote_copy(
            src_ref=back.at[peer],
            dst_ref=out_ref.at[me],
            send_sem=send_b.at[k - 1],
            recv_sem=recv_b.at[k - 1],
            device_id={"seq": peer},
            device_id_type=pl.DeviceIdType.MESH,
        )
        copy.start()
        homeward.append(copy)
    out_ref[me] = back[me]
    for copy in homeward:
        copy.wait()


def entering_states(local_state, grow, pick, first, bank, place, count):
    blocks, rows_all, _ = local_state.shape
    heads = grow.shape[1]
    rows = rows_all // count
    local = local_state.astype(jnp.bfloat16).reshape(blocks, count, rows, STATE)
    local = local.transpose(1, 0, 2, 3)
    if heads < count:
        grow = jnp.repeat(grow, count // heads, axis=1)
    grow = grow.reshape(blocks, count, -1).transpose(1, 0, 2).reshape(count, -1)
    padded = -(-grow.shape[1] // 8) * 8
    grow = jnp.pad(grow, ((0, 0), (0, padded - grow.shape[1])))
    grow = jnp.broadcast_to(grow[:, :, None], (count, padded, STATE))
    picks = jnp.concatenate([1.0 - first[:, None], first[:, None] * pick], axis=1)
    picks = jnp.pad(picks, ((0, 0), (0, 8 - picks.shape[1])))
    picks = jnp.broadcast_to(picks[:, :, None], (count * blocks, 8, STATE))
    mine = lax.dynamic_slice_in_dim(bank, place * rows, rows, axis=1)
    dma = pltpu.SemaphoreType.DMA((count - 1,))
    out = pl.pallas_call(
        functools.partial(exchange_kernel, count, blocks),
        out_shape=jax.ShapeDtypeStruct((count, blocks, rows, STATE), jnp.bfloat16),
        in_specs=[pl.BlockSpec(memory_space=pltpu.VMEM)] * 4,
        out_specs=pl.BlockSpec(memory_space=pltpu.VMEM),
        scratch_shapes=[
            pltpu.VMEM((count, blocks, rows, STATE), jnp.bfloat16),
            pltpu.VMEM((count, blocks, rows, STATE), jnp.bfloat16),
            pltpu.VMEM((count, padded, STATE), jnp.float32),
            dma, dma, dma, dma, dma, dma,
        ],
        compiler_params=pltpu.CompilerParams(collective_id=0, has_side_effects=True),
        name="exchange",
    )(local, grow, picks, mine)
    return out.transpose(1, 0, 2, 3).reshape(blocks, rows_all, STATE)


def swap(value, axis, bit):
    count = lax.axis_size(axis)
    return lax.ppermute(value, axis, [(source, source ^ bit) for source in range(count)])


def gather_columns(hidden, axis, weights):
    mine, (rows, width) = lax.axis_index(axis), hidden.shape
    starts = range(0, rows, BLOCK)
    own = [hidden[start : start + BLOCK] for start in starts]
    far = [swap(part, axis, 2) for part in own]
    near = [swap(part, axis, 1) for part in own]
    far, weights = lax.optimization_barrier((far, weights))
    both = [swap(part, axis, 1) for part in far]
    wholes = []
    for parts in zip(own, near, far, both):
        whole = jnp.zeros((BLOCK, width * 4), hidden.dtype)
        for bits, part in enumerate(parts):
            whole = lax.dynamic_update_slice_in_dim(whole, part, (mine ^ bits) * width, axis=1)
        wholes.append(whole)
    return wholes, weights


def tail_kernel(
    per_group, cum_ref, cum_t_ref, dt_t_ref, xs_ref, bs_ref, cs_ref, gate_ref, state_ref,
    skip_ref, gain_ref, out_ref, y_ref,
):
    tokens, heads = cum_ref.shape[1:]
    lower = lax.broadcasted_iota(jnp.int32, (tokens, tokens), 0) >= lax.broadcasted_iota(
        jnp.int32, (tokens, tokens), 1
    )
    across = (((1,), (1,)), ((), ()))
    wide = per_group * HEAD_DIM
    for group in range(heads // per_group):
        of_group = slice(group * STATE, (group + 1) * STATE)
        channels = slice(group * wide, (group + 1) * wide)
        cs = cs_ref[0, :, of_group]
        scores = lax.dot_general(
            cs, bs_ref[0, :, of_group], across, preferred_element_type=jnp.float32
        )
        y_ref[:, channels] = lax.dot_general(
            cs, state_ref[0, channels, :], across, preferred_element_type=jnp.float32
        )
        for head in range(group * per_group, (group + 1) * per_group):
            here = slice(head * HEAD_DIM, (head + 1) * HEAD_DIM)
            cum = cum_ref[0, :, head : head + 1]
            diff = cum - cum_t_ref[0, head : head + 1, :]
            damp = jnp.exp(jnp.where(lower, diff, -jnp.inf))
            mix = (scores * damp * dt_t_ref[0, head : head + 1, :]).astype(jnp.bfloat16)
            y_ref[:, here] = jnp.exp(cum) * y_ref[:, here] + jnp.dot(
                mix, xs_ref[0, :, here], preferred_element_type=jnp.float32
            )
        gate = gate_ref[0, :, channels].astype(jnp.float32)
        y = y_ref[:, channels] + skip_ref[:, channels] * xs_ref[0, :, channels].astype(jnp.float32)
        gated = y * (gate / (1.0 + jnp.exp(-gate)))
        mean = jnp.mean(gated * gated, axis=1, keepdims=True)
        normed = gated * lax.rsqrt(mean + 1e-05) * gain_ref[:, channels]
        out_ref[0, :, channels] = normed.astype(jnp.bfloat16)


def finish(cum, dt, xs, bs, cs, gate, state_in, skip, gain, per_group):
    blocks, _, inner = xs.shape

    def each(array):
        return pl.BlockSpec((1,) + array.shape[1:], lambda c: (c, 0, 0))

    def fixed(array):
        return pl.BlockSpec(array.shape, lambda c: (0, 0))

    split = (cum, cum.transpose(0, 2, 1), dt.transpose(0, 2, 1), xs, bs, cs, gate, state_in)
    shared = (skip, gain)
    return pl.pallas_call(
        functools.partial(tail_kernel, per_group),
        grid=(blocks,),
        out_shape=jax.ShapeDtypeStruct(xs.shape, jnp.bfloat16),
        in_specs=[each(array) for array in split] + [fixed(array) for array in shared],
        out_specs=each(xs),
        scratch_shapes=[pltpu.VMEM((BLOCK, inner), jnp.float32)],
        compiler_params=pltpu.CompilerParams(vmem_limit_bytes=32 * 1024 * 1024),
        name="finish",
    )(*split, *shared)


def per_device(
    hidden,
    w_zx,
    w_bc,
    w_dt,
    conv_x,
    conv_x_bias,
    conv_bc,
    conv_bc_bias,
    a_log,
    dt_bias,
    d_skip,
    norm_gain,
    state_bank,
    conv_bank_x,
    conv_bank_bc,
    prompt_blocks,
    prompt_order,
    resume_slot,
):
    devices = lax.axis_size("seq")
    place = lax.axis_index("seq")
    rows_dev = hidden.shape[0]
    blocks = rows_dev // BLOCK
    inner_dev = w_zx.shape[2]
    gstate_dev = w_bc.shape[2]
    heads_dev = w_dt.shape[1]
    groups_dev = gstate_dev // STATE
    per_group = heads_dev // groups_dev
    channels = inner_dev + 2 * gstate_dev
    prompts = prompt_blocks.shape[0]
    flat_zx = w_zx.reshape(WIDTH, 2 * inner_dev)
    flat_bc = w_bc.reshape(WIDTH, 2 * gstate_dev)
    pieces, flat_zx = gather_columns(hidden, "mp", flat_zx)
    zx = [
        jnp.dot(piece, flat_zx, preferred_element_type=jnp.float32).astype(jnp.bfloat16)
        for piece in pieces
    ]
    zx, piece = jnp.concatenate(zx, axis=0), jnp.concatenate(pieces, axis=0)
    bc = jnp.dot(piece, flat_bc, preferred_element_type=jnp.float32).astype(jnp.bfloat16)
    dt_raw = jnp.dot(piece, w_dt, preferred_element_type=jnp.float32)
    gate = zx[:, :inner_dev]
    mixin = jnp.concatenate([zx[:, inner_dev:], bc], axis=1).reshape(blocks, BLOCK, channels)
    own_tails = mixin[:, BLOCK - (KERNEL - 1) :, :]
    arrived = from_behind(own_tails, "seq", 1)
    wrapped = jnp.concatenate([jnp.zeros_like(arrived[:1]), arrived[:-1]], axis=0)
    before = jnp.where(place > 0, arrived, wrapped)
    prompt_ids = jnp.arange(prompts, dtype=jnp.int32)
    order_hot = (prompt_order[:, None] == prompt_ids[None, :]).astype(jnp.int32)
    lengths = jnp.sum(order_hot * prompt_blocks[None, :], axis=1)
    slots = jnp.sum(order_hot * resume_slot[None, :], axis=1)
    ends = jnp.cumsum(lengths)
    starts = ends - lengths
    every_id = jnp.arange(blocks * devices, dtype=jnp.int32)
    inside = (
        (every_id[:, None] >= starts[None, :]) & (every_id[:, None] < ends[None, :])
    ).astype(jnp.int32)
    every_slot = jnp.sum(inside * slots[None, :], axis=1)
    every_first = jnp.any(every_id[:, None] == starts[None, :], axis=1).astype(jnp.float32)
    every_pick = (
        every_slot[:, None] == jnp.arange(BANK, dtype=jnp.int32)[None, :]
    ).astype(jnp.float32)
    stream_ids = jnp.arange(blocks, dtype=jnp.int32) * devices + place
    first = jnp.any(stream_ids[:, None] == starts[None, :], axis=1)
    block_slot = jnp.sum(
        jnp.where(stream_ids[:, None] == every_id[None, :], every_slot[None, :], 0), axis=1
    )
    pick = (block_slot[:, None] == jnp.arange(BANK, dtype=jnp.int32)[None, :]).astype(jnp.float32)
    bank_rows = jnp.concatenate(
        [conv_bank_x, conv_bank_bc.reshape(BANK, KERNEL - 1, 2 * gstate_dev)], axis=2
    )
    bank_tail = jnp.einsum("cr,rkz->ckz", pick, bank_rows.astype(jnp.float32)).astype(jnp.bfloat16)
    tail = jnp.where(first[:, None, None], bank_tail, before)
    kernel = jnp.concatenate([conv_x, conv_bc.reshape(KERNEL, 2 * gstate_dev)], axis=1)
    bias = jnp.concatenate([conv_x_bias, conv_bc_bias.reshape(2 * gstate_dev)], axis=0)
    padded = jnp.concatenate([tail, mixin], axis=1).astype(jnp.float32)
    acc = bias[None, None, :] + padded[:, 0:BLOCK] * kernel[0]
    for k in range(1, KERNEL):
        acc = acc + padded[:, k : k + BLOCK] * kernel[k]
    conv = jax.nn.silu(acc).astype(jnp.bfloat16)
    xs = conv[..., :inner_dev].reshape(blocks, BLOCK, groups_dev, per_group, HEAD_DIM)
    bs = conv[..., inner_dev : inner_dev + gstate_dev].reshape(blocks, BLOCK, groups_dev, STATE)
    dt = jax.nn.softplus(dt_raw.reshape(blocks, BLOCK, heads_dev) + dt_bias[None, None, :])
    cum = jnp.cumsum(dt * (-jnp.exp(a_log))[None, None, :], axis=1)
    last = cum[:, -1, :]
    grow = jnp.exp(last)
    factor = (dt * jnp.exp(last[:, None, :] - cum)).reshape(blocks, BLOCK, groups_dev, per_group, 1)
    weighted = (xs.astype(jnp.float32) * factor).astype(jnp.bfloat16)
    local_state = jnp.einsum(
        "cqgjp,cqgn->cgjpn", weighted, bs, preferred_element_type=jnp.float32
    ).reshape(blocks, heads_dev, HEAD_DIM, STATE)
    state_in = entering_states(
        local_state.reshape(blocks, heads_dev * HEAD_DIM, STATE),
        grow,
        every_pick,
        every_first,
        state_bank.reshape(BANK, heads_dev * HEAD_DIM, STATE),
        place,
        devices,
    )
    result = finish(
        cum,
        dt,
        conv[..., :inner_dev],
        conv[..., inner_dev : inner_dev + gstate_dev],
        conv[..., inner_dev + gstate_dev :],
        gate.reshape(blocks, BLOCK, inner_dev),
        state_in,
        jnp.repeat(d_skip, HEAD_DIM)[None, :],
        norm_gain[None, :],
        per_group,
    )
    return result.reshape(rows_dev, inner_dev)


def solution(mesh):
    placed = (
        P("seq", "mp"),
        P(None, None, "mp"),
        P(None, None, "mp"),
        P(None, "mp"),
        P(None, "mp"),
        P("mp"),
        P(None, None, "mp"),
        P(None, "mp"),
        P("mp"),
        P("mp"),
        P("mp"),
        P("mp"),
        P(None, "mp", None, None),
        P(None, None, "mp"),
        P(None, None, None, "mp"),
        P(),
        P(),
        P(),
    )
    return jax.shard_map(
        per_device, mesh=mesh, in_specs=placed, out_specs=P("seq", "mp"), check_vma=False
    )
```

```python
import functools

import jax
import jax.numpy as jnp
from jax import lax
from jax.experimental import pallas as pl
from jax.experimental.pallas import tpu as pltpu
from jax.sharding import PartitionSpec as P

WIDTH = 4096
HEAD_DIM = 64
STATE = 128
BLOCK = 256
KERNEL = 4
BANK = 2


def from_behind(value, axis, steps):
    count = lax.axis_size(axis)
    pairs = [(source, (source + steps) % count) for source in range(count)]
    return lax.ppermute(value, axis, pairs)


def exchange_kernel(
    count, blocks, local_ref, grow_ref, pick_ref, bank_ref, out_ref,
    got, back, grown, send_a, recv_a, send_g, recv_g, send_b, recv_b,
):
    me = lax.axis_index("seq")
    barrier = pltpu.get_barrier_semaphore()
    for k in range(1, count):
        pl.semaphore_signal(
            barrier,
            inc=1,
            device_id={"seq": lax.rem(me + k, count)},
            device_id_type=pl.DeviceIdType.MESH,
        )
    pl.semaphore_wait(barrier, count - 1)
    outward = []
    for k in range(1, count):
        peer = lax.rem(me + k, count)
        for src, dst, send, recv in (
            (grow_ref, grown, send_g, recv_g),
            (local_ref, got, send_a, recv_a),
        ):
            copy = pltpu.make_async_remote_copy(
                src_ref=src.at[peer],
                dst_ref=dst.at[me],
                send_sem=send.at[k - 1],
                recv_sem=recv.at[k - 1],
                device_id={"seq": peer},
                device_id_type=pl.DeviceIdType.MESH,
            )
            copy.start()
            outward.append(copy)
    got[me] = local_ref[me]
    grown[me] = grow_ref[me]
    for copy in outward:
        copy.wait()
    rows = local_ref.shape[2]
    parts = max(rows // HEAD_DIM, 1)
    span = rows // parts
    for part in range(parts):
        here = slice(part * span, (part + 1) * span)
        state = jnp.zeros((span, STATE), jnp.float32)
        for c in range(count * blocks):
            device, row = c % count, c // count
            state = pick_ref[c, 0:1, :] * state
            for r in range(BANK):
                state = state + pick_ref[c, 1 + r : 2 + r, :] * bank_ref[r, here, :]
            back[device, row, here, :] = state.astype(jnp.bfloat16)
            at = row * parts + part
            state = grown[device, at : at + 1, :] * state + got[device, row, here, :].astype(
                jnp.float32
            )
    homeward = []
    for k in range(1, count):
        peer = lax.rem(me + k, count)
        copy = pltpu.make_async_remote_copy(
            src_ref=back.at[peer],
            dst_ref=out_ref.at[me],
            send_sem=send_b.at[k - 1],
            recv_sem=recv_b.at[k - 1],
            device_id={"seq": peer},
            device_id_type=pl.DeviceIdType.MESH,
        )
        copy.start()
        homeward.append(copy)
    out_ref[me] = back[me]
    for copy in homeward:
        copy.wait()


def entering_states(local_state, grow, pick, first, bank, place, count):
    blocks, rows_all, _ = local_state.shape
    heads = grow.shape[1]
    rows = rows_all // count
    local = local_state.astype(jnp.bfloat16).reshape(blocks, count, rows, STATE)
    local = local.transpose(1, 0, 2, 3)
    if heads < count:
        grow = jnp.repeat(grow, count // heads, axis=1)
    grow = grow.reshape(blocks, count, -1).transpose(1, 0, 2).reshape(count, -1)
    padded = -(-grow.shape[1] // 8) * 8
    grow = jnp.pad(grow, ((0, 0), (0, padded - grow.shape[1])))
    grow = jnp.broadcast_to(grow[:, :, None], (count, padded, STATE))
    picks = jnp.concatenate([1.0 - first[:, None], first[:, None] * pick], axis=1)
    picks = jnp.pad(picks, ((0, 0), (0, 8 - picks.shape[1])))
    picks = jnp.broadcast_to(picks[:, :, None], (count * blocks, 8, STATE))
    mine = lax.dynamic_slice_in_dim(bank, place * rows, rows, axis=1)
    dma = pltpu.SemaphoreType.DMA((count - 1,))
    out = pl.pallas_call(
        functools.partial(exchange_kernel, count, blocks),
        out_shape=jax.ShapeDtypeStruct((count, blocks, rows, STATE), jnp.bfloat16),
        in_specs=[pl.BlockSpec(memory_space=pltpu.VMEM)] * 4,
        out_specs=pl.BlockSpec(memory_space=pltpu.VMEM),
        scratch_shapes=[
            pltpu.VMEM((count, blocks, rows, STATE), jnp.bfloat16),
            pltpu.VMEM((count, blocks, rows, STATE), jnp.bfloat16),
            pltpu.VMEM((count, padded, STATE), jnp.float32),
            dma, dma, dma, dma, dma, dma,
        ],
        compiler_params=pltpu.CompilerParams(collective_id=0, has_side_effects=True),
        name="exchange",
    )(local, grow, picks, mine)
    return out.transpose(1, 0, 2, 3).reshape(blocks, rows_all, STATE)


def swap(value, axis, bit):
    count = lax.axis_size(axis)
    return lax.ppermute(value, axis, [(source, source ^ bit) for source in range(count)])


def gather_columns(hidden, axis, weights):
    mine, (rows, width) = lax.axis_index(axis), hidden.shape
    starts = range(0, rows, BLOCK)
    own = [hidden[start : start + BLOCK] for start in starts]
    far = [swap(part, axis, 2) for part in own]
    near = [swap(part, axis, 1) for part in own]
    far, weights = lax.optimization_barrier((far, weights))
    both = [swap(part, axis, 1) for part in far]
    return [part for parts in (own, near, far, both) for part in parts], weights


def project_kernel(blocks, *refs):
    parts, (zx_w, bc_w, dt_w, zx_ref, bc_ref, dt_ref) = refs[: 4 * blocks], refs[4 * blocks :]
    mine, width = lax.axis_index("mp"), parts[0].shape[1]

    def product(weight_ref):
        total = None
        for bits in range(4):
            rows = [part[...] for part in parts[bits * blocks : (bits + 1) * blocks]]
            at = pl.multiple_of((mine ^ bits) * width, width)
            term = jnp.dot(
                jnp.concatenate(rows, axis=0),
                weight_ref[pl.ds(at, width), :],
                preferred_element_type=jnp.float32,
            )
            total = term if total is None else total + term
        return total

    zx_ref[...] = product(zx_w).astype(jnp.bfloat16)

    @pl.when(pl.program_id(0) == 0)
    def _():
        bc_ref[...] = product(bc_w).astype(jnp.bfloat16)
        dt_ref[...] = product(dt_w)


def project(parts, zx_w, bc_w, dt_w):
    blocks, tile = len(parts) // 4, 512
    rows = blocks * BLOCK

    def fixed(shape):
        return pl.BlockSpec(shape, lambda n: (0, 0))

    return pl.pallas_call(
        functools.partial(project_kernel, blocks),
        grid=(zx_w.shape[1] // tile,),
        out_shape=(
            jax.ShapeDtypeStruct((rows, zx_w.shape[1]), jnp.bfloat16),
            jax.ShapeDtypeStruct((rows, bc_w.shape[1]), jnp.bfloat16),
            jax.ShapeDtypeStruct((rows, dt_w.shape[1]), jnp.float32),
        ),
        in_specs=[fixed(part.shape) for part in parts]
        + [pl.BlockSpec((WIDTH, tile), lambda n: (0, n)), fixed(bc_w.shape), fixed(dt_w.shape)],
        out_specs=(
            pl.BlockSpec((rows, tile), lambda n: (0, n)),
            fixed((rows, bc_w.shape[1])),
            fixed((rows, dt_w.shape[1])),
        ),
        compiler_params=pltpu.CompilerParams(vmem_limit_bytes=40 * 1024 * 1024),
        name="project",
    )(*parts, zx_w, bc_w, dt_w)


def tail_kernel(
    per_group, cum_ref, cum_t_ref, dt_t_ref, xs_ref, bs_ref, cs_ref, gate_ref, state_ref,
    skip_ref, gain_ref, out_ref, y_ref,
):
    tokens, heads = cum_ref.shape[1:]
    lower = lax.broadcasted_iota(jnp.int32, (tokens, tokens), 0) >= lax.broadcasted_iota(
        jnp.int32, (tokens, tokens), 1
    )
    across = (((1,), (1,)), ((), ()))
    wide = per_group * HEAD_DIM
    for group in range(heads // per_group):
        of_group = slice(group * STATE, (group + 1) * STATE)
        channels = slice(group * wide, (group + 1) * wide)
        cs = cs_ref[0, :, of_group]
        scores = lax.dot_general(
            cs, bs_ref[0, :, of_group], across, preferred_element_type=jnp.float32
        )
        y_ref[:, channels] = lax.dot_general(
            cs, state_ref[0, channels, :], across, preferred_element_type=jnp.float32
        )
        for head in range(group * per_group, (group + 1) * per_group):
            here = slice(head * HEAD_DIM, (head + 1) * HEAD_DIM)
            cum = cum_ref[0, :, head : head + 1]
            diff = cum - cum_t_ref[0, head : head + 1, :]
            damp = jnp.exp(jnp.where(lower, diff, -jnp.inf))
            mix = (scores * damp * dt_t_ref[0, head : head + 1, :]).astype(jnp.bfloat16)
            y_ref[:, here] = jnp.exp(cum) * y_ref[:, here] + jnp.dot(
                mix, xs_ref[0, :, here], preferred_element_type=jnp.float32
            )
        gate = gate_ref[0, :, channels].astype(jnp.float32)
        y = y_ref[:, channels] + skip_ref[:, channels] * xs_ref[0, :, channels].astype(jnp.float32)
        gated = y * (gate / (1.0 + jnp.exp(-gate)))
        mean = jnp.mean(gated * gated, axis=1, keepdims=True)
        normed = gated * lax.rsqrt(mean + 1e-05) * gain_ref[:, channels]
        out_ref[0, :, channels] = normed.astype(jnp.bfloat16)


def finish(cum, dt, xs, bs, cs, gate, state_in, skip, gain, per_group):
    blocks, _, inner = xs.shape

    def each(array):
        return pl.BlockSpec((1,) + array.shape[1:], lambda c: (c, 0, 0))

    def fixed(array):
        return pl.BlockSpec(array.shape, lambda c: (0, 0))

    split = (cum, cum.transpose(0, 2, 1), dt.transpose(0, 2, 1), xs, bs, cs, gate, state_in)
    shared = (skip, gain)
    return pl.pallas_call(
        functools.partial(tail_kernel, per_group),
        grid=(blocks,),
        out_shape=jax.ShapeDtypeStruct(xs.shape, jnp.bfloat16),
        in_specs=[each(array) for array in split] + [fixed(array) for array in shared],
        out_specs=each(xs),
        scratch_shapes=[pltpu.VMEM((BLOCK, inner), jnp.float32)],
        compiler_params=pltpu.CompilerParams(vmem_limit_bytes=32 * 1024 * 1024),
        name="finish",
    )(*split, *shared)


def per_device(
    hidden,
    w_zx,
    w_bc,
    w_dt,
    conv_x,
    conv_x_bias,
    conv_bc,
    conv_bc_bias,
    a_log,
    dt_bias,
    d_skip,
    norm_gain,
    state_bank,
    conv_bank_x,
    conv_bank_bc,
    prompt_blocks,
    prompt_order,
    resume_slot,
):
    devices = lax.axis_size("seq")
    place = lax.axis_index("seq")
    rows_dev = hidden.shape[0]
    blocks = rows_dev // BLOCK
    inner_dev = w_zx.shape[2]
    gstate_dev = w_bc.shape[2]
    heads_dev = w_dt.shape[1]
    groups_dev = gstate_dev // STATE
    per_group = heads_dev // groups_dev
    channels = inner_dev + 2 * gstate_dev
    prompts = prompt_blocks.shape[0]
    flat_zx = w_zx.reshape(WIDTH, 2 * inner_dev)
    flat_bc = w_bc.reshape(WIDTH, 2 * gstate_dev)
    pieces, flat_zx = gather_columns(hidden, "mp", flat_zx)
    zx, bc, dt_raw = project(pieces, flat_zx, flat_bc, w_dt)
    gate = zx[:, :inner_dev]
    mixin = jnp.concatenate([zx[:, inner_dev:], bc], axis=1).reshape(blocks, BLOCK, channels)
    own_tails = mixin[:, BLOCK - (KERNEL - 1) :, :]
    arrived = from_behind(own_tails, "seq", 1)
    wrapped = jnp.concatenate([jnp.zeros_like(arrived[:1]), arrived[:-1]], axis=0)
    before = jnp.where(place > 0, arrived, wrapped)
    prompt_ids = jnp.arange(prompts, dtype=jnp.int32)
    order_hot = (prompt_order[:, None] == prompt_ids[None, :]).astype(jnp.int32)
    lengths = jnp.sum(order_hot * prompt_blocks[None, :], axis=1)
    slots = jnp.sum(order_hot * resume_slot[None, :], axis=1)
    ends = jnp.cumsum(lengths)
    starts = ends - lengths
    every_id = jnp.arange(blocks * devices, dtype=jnp.int32)
    inside = (
        (every_id[:, None] >= starts[None, :]) & (every_id[:, None] < ends[None, :])
    ).astype(jnp.int32)
    every_slot = jnp.sum(inside * slots[None, :], axis=1)
    every_first = jnp.any(every_id[:, None] == starts[None, :], axis=1).astype(jnp.float32)
    every_pick = (
        every_slot[:, None] == jnp.arange(BANK, dtype=jnp.int32)[None, :]
    ).astype(jnp.float32)
    stream_ids = jnp.arange(blocks, dtype=jnp.int32) * devices + place
    first = jnp.any(stream_ids[:, None] == starts[None, :], axis=1)
    block_slot = jnp.sum(
        jnp.where(stream_ids[:, None] == every_id[None, :], every_slot[None, :], 0), axis=1
    )
    pick = (block_slot[:, None] == jnp.arange(BANK, dtype=jnp.int32)[None, :]).astype(jnp.float32)
    bank_rows = jnp.concatenate(
        [conv_bank_x, conv_bank_bc.reshape(BANK, KERNEL - 1, 2 * gstate_dev)], axis=2
    )
    bank_tail = jnp.einsum("cr,rkz->ckz", pick, bank_rows.astype(jnp.float32)).astype(jnp.bfloat16)
    tail = jnp.where(first[:, None, None], bank_tail, before)
    kernel = jnp.concatenate([conv_x, conv_bc.reshape(KERNEL, 2 * gstate_dev)], axis=1)
    bias = jnp.concatenate([conv_x_bias, conv_bc_bias.reshape(2 * gstate_dev)], axis=0)
    padded = jnp.concatenate([tail, mixin], axis=1).astype(jnp.float32)
    acc = bias[None, None, :] + padded[:, 0:BLOCK] * kernel[0]
    for k in range(1, KERNEL):
        acc = acc + padded[:, k : k + BLOCK] * kernel[k]
    conv = jax.nn.silu(acc).astype(jnp.bfloat16)
    xs = conv[..., :inner_dev].reshape(blocks, BLOCK, groups_dev, per_group, HEAD_DIM)
    bs = conv[..., inner_dev : inner_dev + gstate_dev].reshape(blocks, BLOCK, groups_dev, STATE)
    dt = jax.nn.softplus(dt_raw.reshape(blocks, BLOCK, heads_dev) + dt_bias[None, None, :])
    cum = jnp.cumsum(dt * (-jnp.exp(a_log))[None, None, :], axis=1)
    last = cum[:, -1, :]
    grow = jnp.exp(last)
    factor = (dt * jnp.exp(last[:, None, :] - cum)).reshape(blocks, BLOCK, groups_dev, per_group, 1)
    weighted = (xs.astype(jnp.float32) * factor).astype(jnp.bfloat16)
    local_state = jnp.einsum(
        "cqgjp,cqgn->cgjpn", weighted, bs, preferred_element_type=jnp.float32
    ).reshape(blocks, heads_dev, HEAD_DIM, STATE)
    state_in = entering_states(
        local_state.reshape(blocks, heads_dev * HEAD_DIM, STATE),
        grow,
        every_pick,
        every_first,
        state_bank.reshape(BANK, heads_dev * HEAD_DIM, STATE),
        place,
        devices,
    )
    result = finish(
        cum,
        dt,
        conv[..., :inner_dev],
        conv[..., inner_dev : inner_dev + gstate_dev],
        conv[..., inner_dev + gstate_dev :],
        gate.reshape(blocks, BLOCK, inner_dev),
        state_in,
        jnp.repeat(d_skip, HEAD_DIM)[None, :],
        norm_gain[None, :],
        per_group,
    )
    return result.reshape(rows_dev, inner_dev)


def solution(mesh):
    placed = (
        P("seq", "mp"),
        P(None, None, "mp"),
        P(None, None, "mp"),
        P(None, "mp"),
        P(None, "mp"),
        P("mp"),
        P(None, None, "mp"),
        P(None, "mp"),
        P("mp"),
        P("mp"),
        P("mp"),
        P("mp"),
        P(None, "mp", None, None),
        P(None, None, "mp"),
        P(None, None, None, "mp"),
        P(),
        P(),
        P(),
    )
    return jax.shard_map(
        per_device, mesh=mesh, in_specs=placed, out_specs=P("seq", "mp"), check_vma=False
    )
```
